128 devices in a mesh: frame: 32 (over z, y, x_lo), head: 4 (over x_hi, core).
Axes of the slice: x: 4 (x_hi: 2, x_lo: 2; x = x_hi * 2 + x_lo), y: 4, z: 4, core: 2. Of those that a mesh axis runs over, the one named last changes fastest.
Arguments:
- queries: bfloat16 [24576, 3072], P(('frame', 'head')), may hold values from -4.5 to 4.5
- keys: bfloat16 [24576, 3072], P(('frame', 'head')), may hold values from -4.5 to 4.5
- values: bfloat16 [24576, 3072], P(('frame', 'head')), may hold values from -6 to 6
- grad_out: bfloat16 [24576, 3072], P(('frame', 'head')), may hold values from -6 to 6
- neighbours: int32 [64, 9], P('frame'), may hold values from -1 to 63, as said below
Outputs:
- grad_queries: bfloat16 [24576, 3072], P(('frame', 'head'))
- grad_keys: bfloat16 [24576, 3072], P(('frame', 'head'))
- grad_values: bfloat16 [24576, 3072], P(('frame', 'head'))
The draws below stay inside these ranges and needn't reach their ends.
Inputs may be any that keep to these rules, and one draw needn't show every extreme that they name: neighbours[i, 3 (dt + 1) + (dw + 1)] for dt, dw in -1, 0, 1 is the tile in time-tile row i // 2 + dt and column i % 2 + dw when that row exists and lies in the same clip and the column lies in 0 to 1, else -1. Clips are runs of whole time-tile rows drawn from the seed; the first and last rows end clips. No tile is listed twice in a row, and slot 4 is tile i itself.
All inputs are finite; a program needn't handle non-finite values.
Results may differ from the reference program's by a relative error of at most 0.018.
Values may be sent and summed in bfloat16 or wider, within the bound.
A program may use at most 192 MiB of HBM per device.

```python
import jax
import jax.numpy as jnp
from jax import lax

HEADS = 24
D_HEAD = 128
TILE = 384
SLOTS = 9
TW = 2
TILES = 64
TOKENS = 24576


def draw_queries(key, part):
    key = jax.random.fold_in(key, 5)
    return jnp.clip(jax.random.normal(key, (TOKENS, HEADS * D_HEAD), jnp.float32), -4.5, 4.5).astype(jnp.bfloat16)


def draw_keys(key, part):
    key = jax.random.fold_in(key, 7)
    return jnp.clip(jax.random.normal(key, (TOKENS, HEADS * D_HEAD), jnp.float32), -4.5, 4.5).astype(jnp.bfloat16)


def draw_neighbours(key, part):
    key = jax.random.fold_in(key, 11)
    row_count = TILES // TW
    cuts = jax.random.randint(key, (row_count - 1,), 0, 4) == 0
    edges = jnp.concatenate([jnp.array([True]), cuts, jnp.array([True])])
    tile_ids = jnp.arange(TILES).astype(jnp.int32)
    row_of = tile_ids // TW
    col_of = tile_ids % TW
    columns = []
    for shift_t in (-1, 0, 1):
        for shift_w in (-1, 0, 1):
            target_row = row_of + shift_t
            target_col = col_of + shift_w
            inside = (target_row >= 0) & (target_row < row_count) & (target_col >= 0) & (target_col < TW)
            if shift_t == -1:
                inside = inside & jnp.logical_not(edges[row_of])
            if shift_t == 1:
                inside = inside & jnp.logical_not(edges[row_of + 1])
            columns.append(jnp.where(inside, target_row * TW + target_col, -1))
    return jnp.stack(columns, axis=1).astype(jnp.int32)


def steps_of(key, dims, split, least, high):
    def one(dim, blocks):
        heights = jax.random.uniform(jax.random.fold_in(jax.random.fold_in(key, 6), dim), (blocks,), jnp.float32, least / len(split), high / len(split))
        return jnp.repeat(jnp.exp(heights), dims[dim] // blocks).reshape((-1,) + (1,) * (len(dims) - dim - 1))

    loudness = one(*split[0])
    for cut in split[1:]:
        loudness = loudness * one(*cut)
    return loudness


def bell_draw(key, shape, scale, reach, shards=(), held_as=jnp.bfloat16):
    values = scale * jax.random.normal(key, shape, jnp.float32)
    if shards:
        values = values * steps_of(key, shape, shards, -0.22, 0.18)
    return jnp.clip(values, -reach, reach).astype(held_as)


def setup_inputs(seed: int = 0) -> dict:
    arg_keys = jax.random.split(jax.random.key(seed), 6)
    queries = draw_queries(jax.random.fold_in(arg_keys[5], 71), 0)
    keys = draw_keys(jax.random.fold_in(arg_keys[5], 71), 0)
    values = bell_draw(arg_keys[2], (TOKENS, HEADS * D_HEAD), 1.0, 6.0, ((0, 128),))
    grad_out = bell_draw(arg_keys[3], (TOKENS, HEADS * D_HEAD), 1.0, 6.0, ((0, 128),))
    neighbours = draw_neighbours(jax.random.fold_in(arg_keys[5], 71), 0)
    return dict(queries=queries, keys=keys, values=values, grad_out=grad_out, neighbours=neighbours)


def head_terms(query_tile, grad_tile, key_rows, value_rows, position, present):
    scale = D_HEAD ** -0.5
    highest = lax.Precision.HIGHEST
    tile_cols = position.shape[0]
    key_tiles = jnp.take(key_rows, position, axis=0).reshape(tile_cols, -1, D_HEAD).astype(jnp.float32)
    value_tiles = jnp.take(value_rows, position, axis=0).reshape(tile_cols, -1, D_HEAD).astype(jnp.float32)
    allowed = jnp.repeat(present, TILE, axis=1)[:, None, :]
    query_wide = query_tile.astype(jnp.float32)
    grad_wide = grad_tile.astype(jnp.float32)
    scores = jnp.einsum('tqd,tkd->tqk', query_wide, key_tiles, precision=highest) * scale
    scores = jnp.where(allowed, scores, -jnp.inf)
    expon = jnp.exp(scores - jnp.max(scores, axis=-1, keepdims=True))
    probs = expon / jnp.sum(expon, axis=-1, keepdims=True)
    probs_low = probs.astype(jnp.bfloat16).astype(jnp.float32)
    dprobs = jnp.einsum('tqd,tkd->tqk', grad_wide, value_tiles, precision=highest)
    row_dot = jnp.sum(probs * dprobs, axis=-1, keepdims=True)
    dscores = (probs * (dprobs - row_dot)).astype(jnp.bfloat16).astype(jnp.float32)
    query_grad = jnp.einsum('tqk,tkd->tqd', dscores, key_tiles, precision=highest) * scale
    key_slot = jnp.einsum('tqk,tqd->tkd', dscores, query_wide, precision=highest) * scale
    value_slot = jnp.einsum('tqk,tqd->tkd', probs_low, grad_wide, precision=highest)
    count = key_rows.shape[0]
    onehot = ((position.reshape(-1)[:, None] == jnp.arange(count).astype(jnp.int32)[None, :])
              & present.reshape(-1)[:, None]).astype(jnp.float32)
    key_grad = jnp.einsum('sn,sid->nid', onehot, key_slot.reshape(-1, TILE, D_HEAD), precision=highest)
    value_grad = jnp.einsum('sn,sid->nid', onehot, value_slot.reshape(-1, TILE, D_HEAD), precision=highest)
    return query_grad, key_grad, value_grad


def sent_part(part):
    return lax.optimization_barrier(part.astype(jnp.bfloat16)).astype(jnp.float32)


def reference(queries, keys, values, grad_out, neighbours):
    row_count = TILES // TW

    def tiled(array):
        return array.reshape(row_count, TW, TILE, HEADS, D_HEAD)

    empty = jnp.zeros((1, TW, TILE, HEADS, D_HEAD), jnp.bfloat16)
    keys_padded = jnp.concatenate([empty, tiled(keys), empty], axis=0)
    values_padded = jnp.concatenate([empty, tiled(values), empty], axis=0)
    lists = neighbours.reshape(row_count, TW, SLOTS)
    start = jnp.zeros((row_count + 2, 3 * TW // 3, TILE, HEADS, D_HEAD), jnp.float32)

    def one_row(carry, items):
        key_acc, value_acc = carry
        query_row, grad_row, listing, row_index = items
        key_ext = lax.dynamic_slice_in_dim(keys_padded, row_index, 3, 0).reshape(3 * TW, TILE, HEADS, D_HEAD)
        value_ext = lax.dynamic_slice_in_dim(values_padded, row_index, 3, 0).reshape(3 * TW, TILE, HEADS, D_HEAD)
        present = listing >= 0
        position = jnp.where(present, listing - (row_index - 1) * TW, 0).astype(jnp.int32)

        def per_head(stack):
            return head_terms(stack[0], stack[1], stack[2], stack[3], position, present)

        query_grad, key_grad, value_grad = lax.map(per_head, (
            query_row.transpose(2, 0, 1, 3), grad_row.transpose(2, 0, 1, 3),
            key_ext.transpose(2, 0, 1, 3), value_ext.transpose(2, 0, 1, 3)))
        key_parts = key_grad.transpose(1, 2, 0, 3).reshape(3, TW, TILE, HEADS, D_HEAD)
        value_parts = value_grad.transpose(1, 2, 0, 3).reshape(3, TW, TILE, HEADS, D_HEAD)
        key_parts = jnp.stack([sent_part(key_parts[0]), key_parts[1], sent_part(key_parts[2])])
        value_parts = jnp.stack([sent_part(value_parts[0]), value_parts[1], sent_part(value_parts[2])])
        key_acc = lax.dynamic_update_slice_in_dim(
            key_acc, lax.dynamic_slice_in_dim(key_acc, row_index, 3, 0) + key_parts, row_index, 0)
        value_acc = lax.dynamic_update_slice_in_dim(
            value_acc, lax.dynamic_slice_in_dim(value_acc, row_index, 3, 0) + value_parts, row_index, 0)
        query_out = query_grad.transpose(1, 2, 0, 3).astype(jnp.bfloat16)
        return (key_acc, value_acc), query_out

    (key_acc, value_acc), query_rows = lax.scan(
        one_row, (start, start),
        (tiled(queries), tiled(grad_out), lists, jnp.arange(row_count).astype(jnp.int32)))
    grad_queries = query_rows.reshape(TOKENS, HEADS * D_HEAD)
    grad_keys = key_acc[1:-1].astype(jnp.bfloat16).reshape(TOKENS, HEADS * D_HEAD)
    grad_values = value_acc[1:-1].astype(jnp.bfloat16).reshape(TOKENS, HEADS * D_HEAD)
    return (grad_queries, grad_keys, grad_values)
```

```python
import functools

import jax
import jax.numpy as jnp
from jax import lax
from jax.experimental import pallas as pl
from jax.experimental.pallas import tpu as pltpu
from jax.sharding import PartitionSpec as P

D = 128
ROW = 768
PIECE = 192
MINE = 3
RING = 8
CHUNK = 256
SCALE = D**-0.5
LOG2E = 1.4426950408889634
ABSENT = -1e30
f32 = jnp.float32
bf16 = jnp.bfloat16
MESH = pl.DeviceIdType.MESH


def dot(a, b, dim_a, dim_b):
    return lax.dot_general(a, b, (((dim_a,), (dim_b,)), ((), ())), preferred_element_type=f32)


def wait_bytes(ref, sem):
    pltpu.make_async_copy(ref, ref, sem).wait()


def kernel(
    q_in, k_in, v_in, o_in, near_in,
    q_out, k_out, v_out,
    kb, vb, qb, ob, near, kt, expon, dprob, k_acc, v_acc,
    part_out, part_in, q_res, k_res, v_res,
    near_sem, in_recv, in_send, halo_recv, halo_send, part_recv, part_send, out_recv, out_send,
):
    frame, head = lax.axis_index("frame"), lax.axis_index("head")
    pair, low = frame // 2, frame % 2
    pairs = lax.axis_size("frame") // 2
    me = ((head // 2) * 2 + low) * 2 + head % 2

    def ring_device(index):
        x, core = index // 2, index % 2
        return (pair * 2 + x % 2, (x // 2) * 2 + core)

    def token_start(index):
        x, core = index // 2, index % 2
        return pl.multiple_of((x % 2) * ROW + ((x // 2) * 2 + core) * PIECE, PIECE)

    prev_device = (lax.rem(pair + pairs - 1, pairs) * 2 + low, head)
    next_device = (lax.rem(pair + 1, pairs) * 2 + low, head)
    partner = (pair * 2 + 1 - low, head)

    barrier = pltpu.get_barrier_semaphore()

    def greet(step, carry):
        pl.semaphore_signal(
            barrier, inc=1, device_id=ring_device(lax.rem(me + step, RING)), device_id_type=MESH
        )
        return carry

    lax.fori_loop(1, RING, greet, 0)
    for device in (prev_device, next_device):
        pl.semaphore_signal(barrier, inc=1, device_id=device, device_id_type=MESH)
    pl.semaphore_wait(barrier, RING + 1)

    own_start = token_start(me)
    inputs = ((k_in, kb, ROW), (v_in, vb, ROW), (q_in, qb, 0), (o_in, ob, 0))

    def in_slot(array):
        return 2 * array + low if array < 2 else 2 + array

    def send_inputs(hh, arrays):
        for array in arrays:
            src, dst, shift = inputs[array]
            into = dst.at[hh, pl.ds(pl.multiple_of(shift + own_start, PIECE), PIECE)]
            recv = in_recv.at[hh, in_slot(array)]

            def columns(index):
                return src.at[:, pl.ds(pl.multiple_of((index * MINE + hh) * D, D), D)]

            def send(step, carry):
                there = lax.rem(me + step, RING)
                pltpu.make_async_remote_copy(
                    src_ref=columns(there),
                    dst_ref=into,
                    send_sem=in_send.at[hh, array],
                    recv_sem=recv,
                    device_id=ring_device(there),
                    device_id_type=MESH,
                ).start()
                return carry

            lax.fori_loop(1, RING, send, 0)
            pltpu.make_async_copy(columns(me), into, recv).start()

    def wait_inputs_sent(hh, arrays):
        for array in arrays:
            wait_bytes(kb.at[0, pl.ds(0, (RING - 1) * PIECE)], in_send.at[hh, array])

    def halo_copy(hh, which, side):
        buffer = (kb, vb)[which]
        return pltpu.make_async_remote_copy(
            src_ref=buffer.at[hh, pl.ds(ROW * (1 + side), ROW)],
            dst_ref=buffer.at[hh, pl.ds(ROW * 3 * (1 - side), ROW)],
            send_sem=halo_send.at[hh, 2 * which + side],
            recv_sem=halo_recv.at[hh, 2 * which + side],
            device_id=(prev_device, next_device)[side],
            device_id_type=MESH,
        )

    def send_halo(hh):
        for which in range(2):
            for side in range(2):
                wait_bytes(
                    (kb, vb)[which].at[hh, pl.ds(ROW * (1 + side), ROW)],
                    in_recv.at[hh, 2 * which + side],
                )
                halo_copy(hh, which, side).start()

    def wait_head(hh):
        wait_bytes(qb.at[hh], in_recv.at[hh, 4])
        wait_bytes(ob.at[hh], in_recv.at[hh, 5])
        for which in range(2):
            for side in range(2):
                halo_copy(hh, which, side).wait_recv()

    def part_copy(hh, which, side):
        return pltpu.make_async_remote_copy(
            src_ref=part_out.at[hh, which, side],
            dst_ref=part_in.at[hh, which, side],
            send_sem=part_send.at[hh, 2 * which + side],
            recv_sem=part_recv.at[hh, 2 * which + side],
            device_id=(prev_device, next_device)[side],
            device_id_type=MESH,
        )

    def send_parts(hh):
        for which in range(2):
            for side in range(2):
                part = (k_acc, v_acc)[which][hh, ROW * 3 * side : ROW * 3 * side + ROW, :]
                if which == 0:
                    part = part * SCALE
                part_out[hh, which, side] = part.astype(bf16)
                part_copy(hh, which, side).start()

    results = ((q_res, q_out), (k_res, k_out), (v_res, v_out))

    def send_result(hh, array):
        src, dst = results[array]
        into = dst.at[:, pl.ds(pl.multiple_of((me * MINE + hh) * D, D), D)]

        def rows(index):
            return src.at[hh, pl.ds(token_start(index), PIECE)]

        def send(step, carry):
            there = lax.rem(me + step, RING)
            pltpu.make_async_remote_copy(
                src_ref=rows(there),
                dst_ref=into,
                send_sem=out_send.at[hh, array],
                recv_sem=out_recv.at[array],
                device_id=ring_device(there),
                device_id_type=MESH,
            ).start()
            return carry

        lax.fori_loop(1, RING, send, 0)
        pltpu.make_async_copy(rows(me), into, out_recv.at[array]).start()

    def finish_head(hh):
        for which in range(2):
            for side in range(2):
                part_copy(hh, which, side).wait_recv()
                rows = ROW * (2 - side)
                total = (k_acc, v_acc)[which][hh, rows : rows + ROW, :]
                if which == 0:
                    total = total * SCALE
                total = total + part_in[hh, which, side].astype(f32)
                (k_res, v_res)[which][hh, rows - ROW : rows, :] = total.astype(bf16)
            send_result(hh, 1 + which)

    def attend(hh, row):
        queries = qb[hh, pl.ds(pl.multiple_of(row * ROW, ROW), ROW), :]
        grads = ob[hh, pl.ds(pl.multiple_of(row * ROW, ROW), ROW), :]
        listed = near[row, 0:1, :]
        bias = [
            jnp.where(listed[:, 1:2] >= 0, 0.0, ABSENT).astype(f32),
            None,
            jnp.where(listed[:, 7:8] >= 0, 0.0, ABSENT).astype(f32),
        ]
        chunks = 3 * ROW // CHUNK

        def keys_at(chunk):
            return pl.ds(pl.multiple_of(row * ROW + chunk * CHUNK, CHUNK), CHUNK)

        tops, sums, dots = [], [], []
        for chunk in range(chunks):
            scores = dot(kb[hh, keys_at(chunk), :], queries, 1, 1)
            dprobs = dot(vb[hh, keys_at(chunk), :], grads, 1, 1)
            top = jnp.max(scores, axis=0, keepdims=True)
            weights = jnp.exp2((scores - top) * (SCALE * LOG2E))
            sums.append(jnp.sum(weights, axis=0, keepdims=True))
            dots.append(jnp.sum(weights * dprobs, axis=0, keepdims=True))
            expon[chunk] = weights
            dprob[chunk] = dprobs
            shift = bias[chunk * CHUNK // ROW]
            tops.append(top if shift is None else top + shift)
        top = functools.reduce(jnp.maximum, tops)
        factors = [jnp.exp2((t - top) * (SCALE * LOG2E)) for t in tops]
        total = functools.reduce(jnp.add, [f * s for f, s in zip(factors, sums)])
        inverse = 1.0 / total
        row_dot = functools.reduce(jnp.add, [f * d for f, d in zip(factors, dots)]) * inverse
        query_grad = jnp.zeros((D, ROW), f32)
        for chunk in range(chunks):
            probs = expon[chunk] * (factors[chunk] * inverse)
            dscores = (probs * (dprob[chunk] - row_dot)).astype(bf16)
            v_acc[hh, keys_at(chunk), :] += dot(probs.astype(bf16), grads, 1, 0)
            k_acc[hh, keys_at(chunk), :] += dot(dscores, queries, 1, 0)
            query_grad += dot(kt[:, keys_at(chunk)], dscores, 1, 0)
        q_res[hh, pl.ds(pl.multiple_of(row * ROW, ROW), ROW), :] = (
            (query_grad * SCALE).T.astype(bf16)
        )

    send_inputs(0, (0, 1, 2, 3))
    near_copy = pltpu.make_async_remote_copy(
        src_ref=near_in,
        dst_ref=near.at[low],
        send_sem=near_sem.at[0],
        recv_sem=near_sem.at[1],
        device_id=partner,
        device_id_type=MESH,
    )
    near_copy.start()
    own_near = pltpu.make_async_copy(near_in, near.at[low], near_sem.at[2])
    own_near.start()
    send_inputs(1, (0, 1, 2, 3))
    send_inputs(2, (0, 1, 2, 3))
    k_acc[...] = jnp.zeros_like(k_acc)
    v_acc[...] = jnp.zeros_like(v_acc)
    send_halo(0)
    near_copy.wait()
    own_near.wait()

    def step(index, carry):
        hh, row = index // 2, index % 2

        @pl.when(row == 0)
        def _():
            wait_head(hh)
            kt[...] = kb[hh].T

        attend(hh, row)

        @pl.when(jnp.logical_and(row == 0, hh < MINE - 1))
        def _():
            send_halo(hh + 1)

        @pl.when(jnp.logical_and(row == 0, hh > 0))
        def _():
            finish_head(hh - 1)

        @pl.when(row == 1)
        def _():
            send_parts(hh)
            send_result(hh, 0)

        return carry

    lax.fori_loop(0, 2 * MINE, step, 0)
    finish_head(MINE - 1)

    def drain(hh, carry):
        wait_inputs_sent(hh, (0, 1, 2, 3))
        for which in range(2):
            for side in range(2):
                halo_copy(hh, which, side).wait_send()
                part_copy(hh, which, side).wait_send()
        for array in range(3):
            wait_bytes(kb.at[0, pl.ds(0, (RING - 1) * PIECE)], out_send.at[hh, array])
        return carry

    lax.fori_loop(0, MINE, drain, 0)
    for array in range(3):
        wait_bytes(results[array][1], out_recv.at[array])


def per_device(queries, keys, values, grad_out, neighbours):
    vmem, sem = pltpu.VMEM, pltpu.SemaphoreType.DMA
    out = jax.ShapeDtypeStruct(queries.shape, bf16)
    anywhere = pl.BlockSpec(memory_space=pl.ANY)
    chunks = 3 * ROW // CHUNK
    return pl.pallas_call(
        kernel,
        out_shape=(out, out, out),
        in_specs=[anywhere] * 4 + [pl.BlockSpec(memory_space=vmem)],
        out_specs=(anywhere, anywhere, anywhere),
        scratch_shapes=[
            vmem((MINE, 4 * ROW, D), bf16),
            vmem((MINE, 4 * ROW, D), bf16),
            vmem((MINE, 2 * ROW, D), bf16),
            vmem((MINE, 2 * ROW, D), bf16),
            vmem((2,) + neighbours.shape, jnp.int32),
            vmem((D, 4 * ROW), bf16),
            vmem((chunks, CHUNK, ROW), f32),
            vmem((chunks, CHUNK, ROW), f32),
            vmem((MINE, 4 * ROW, D), f32),
            vmem((MINE, 4 * ROW, D), f32),
            vmem((MINE, 2, 2, ROW, D), bf16),
            vmem((MINE, 2, 2, ROW, D), bf16),
            vmem((MINE, 2 * ROW, D), bf16),
            vmem((MINE, 2 * ROW, D), bf16),
            vmem((MINE, 2 * ROW, D), bf16),
            sem((3,)),
            sem((MINE, 6)),
            sem((MINE, 4)),
            sem((MINE, 4)),
            sem((MINE, 4)),
            sem((MINE, 4)),
            sem((MINE, 4)),
            sem((3,)),
            sem((MINE, 3)),
        ],
        compiler_params=pltpu.CompilerParams(
            collective_id=0, has_side_effects=True, vmem_limit_bytes=56 << 20
        ),
        cost_estimate=pl.CostEstimate(
            flops=13_600_000_000, bytes_accessed=16_000_000, transcendentals=10_600_000
        ),
    )(queries, keys, values, grad_out, neighbours)


def solution(mesh):
    tokens = P(("frame", "head"), None)
    return jax.shard_map(
        per_device,
        mesh=mesh,
        in_specs=(tokens, tokens, tokens, tokens, P("frame", None)),
        out_specs=(tokens, tokens, tokens),
        check_vma=False,
    )
```

```python
import functools

import jax
import jax.numpy as jnp
from jax import lax
from jax.experimental import pallas as pl
from jax.experimental.pallas import tpu as pltpu
from jax.sharding import PartitionSpec as P

D = 128
ROW = 768
PIECE = 192
MINE = 3
RING = 8
CHUNK = 256
SCALE = D**-0.5
LOG2E = 1.4426950408889634
ABSENT = -1e30
f32 = jnp.float32
bf16 = jnp.bfloat16
MESH = pl.DeviceIdType.MESH


def dot(a, b, dim_a, dim_b):
    return lax.dot_general(a, b, (((dim_a,), (dim_b,)), ((), ())), preferred_element_type=f32)


def wait_bytes(ref, sem):
    pltpu.make_async_copy(ref, ref, sem).wait()


def kernel(
    q_in, k_in, v_in, o_in, near_in,
    q_out, k_out, v_out,
    kb, vb, qb, ob, near, kt, expon, dprob, k_acc, v_acc,
    part_out, part_in, q_res, k_res, v_res,
    near_sem, in_recv, in_send, halo_recv, halo_send, part_recv, part_send, out_recv, out_send, entered,
):
    frame, head = lax.axis_index("frame"), lax.axis_index("head")
    pair, low = frame // 2, frame % 2
    pairs = lax.axis_size("frame") // 2
    me = ((head // 2) * 2 + low) * 2 + head % 2

    def ring_device(index):
        x, core = index // 2, index % 2
        return (pair * 2 + x % 2, (x // 2) * 2 + core)

    def token_start(index):
        x, core = index // 2, index % 2
        return pl.multiple_of((x % 2) * ROW + ((x // 2) * 2 + core) * PIECE, PIECE)

    prev_device = (lax.rem(pair + pairs - 1, pairs) * 2 + low, head)
    next_device = (lax.rem(pair + 1, pairs) * 2 + low, head)
    partner = (pair * 2 + 1 - low, head)

    barrier = pltpu.get_barrier_semaphore()
    core = head % 2
    peer_device = ring_device(me + 1 - 2 * core)

    def greet(chip, carry):
        @pl.when(2 * chip != me)
        def _():
            pl.semaphore_signal(
                barrier, inc=1, device_id=ring_device(2 * chip), device_id_type=MESH
            )

        return carry

    lax.fori_loop(0, RING // 2, greet, 0)
    for there in (prev_device, next_device):
        pl.semaphore_signal(
            barrier, inc=1, device_id=(there[0], head + 1 - core), device_id_type=MESH
        )

    @pl.when(core == 0)
    def _():
        pl.semaphore_signal(barrier, inc=1, device_id=peer_device, device_id_type=MESH)
        pl.semaphore_wait(barrier, RING - 1)
        pl.semaphore_signal(entered, inc=1, device_id=peer_device, device_id_type=MESH)

    @pl.when(core == 1)
    def _():
        pl.semaphore_wait(entered, 1)

    def wait_groups():
        @pl.when(core == 1)
        def _():
            pl.semaphore_wait(barrier, 5)
            pl.semaphore_signal(entered, inc=1, device_id=peer_device, device_id_type=MESH)

        @pl.when(core == 0)
        def _():
            pl.semaphore_wait(entered, 1)

    own_start = token_start(me)
    inputs = ((k_in, kb, ROW), (v_in, vb, ROW), (q_in, qb, 0), (o_in, ob, 0))

    def in_slot(array):
        return 2 * array + low if array < 2 else 2 + array

    def send_inputs(hh, arrays):
        for array in arrays:
            src, dst, shift = inputs[array]
            into = dst.at[hh, pl.ds(pl.multiple_of(shift + own_start, PIECE), PIECE)]
            recv = in_recv.at[hh, in_slot(array)]

            def columns(index):
                return src.at[:, pl.ds(pl.multiple_of((index * MINE + hh) * D, D), D)]

            def send(step, carry):
                there = lax.rem(me + step, RING)
                pltpu.make_async_remote_copy(
                    src_ref=columns(there),
                    dst_ref=into,
                    send_sem=in_send.at[hh, array],
                    recv_sem=recv,
                    device_id=ring_device(there),
                    device_id_type=MESH,
                ).start()
                return carry

            lax.fori_loop(1, RING, send, 0)
            pltpu.make_async_copy(columns(me), into, recv).start()

    def wait_inputs_sent(hh, arrays):
        for array in arrays:
            wait_bytes(kb.at[0, pl.ds(0, (RING - 1) * PIECE)], in_send.at[hh, array])

    def halo_copy(hh, which, side):
        buffer = (kb, vb)[which]
        return pltpu.make_async_remote_copy(
            src_ref=buffer.at[hh, pl.ds(ROW * (1 + side), ROW)],
            dst_ref=buffer.at[hh, pl.ds(ROW * 3 * (1 - side), ROW)],
            send_sem=halo_send.at[hh, 2 * which + side],
            recv_sem=halo_recv.at[hh, 2 * which + side],
            device_id=(prev_device, next_device)[side],
            device_id_type=MESH,
        )

    def send_halo(hh):
        for which in range(2):
            for side in range(2):
                wait_bytes(
                    (kb, vb)[which].at[hh, pl.ds(ROW * (1 + side), ROW)],
                    in_recv.at[hh, 2 * which + side],
                )
                halo_copy(hh, which, side).start()

    def wait_head(hh):
        wait_bytes(qb.at[hh], in_recv.at[hh, 4])
        wait_bytes(ob.at[hh], in_recv.at[hh, 5])
        for which in range(2):
            for side in range(2):
                halo_copy(hh, which, side).wait_recv()

    def part_copy(hh, which, side):
        return pltpu.make_async_remote_copy(
            src_ref=part_out.at[hh, which, side],
            dst_ref=part_in.at[hh, which, side],
            send_sem=part_send.at[hh, 2 * which + side],
            recv_sem=part_recv.at[hh, 2 * which + side],
            device_id=(prev_device, next_device)[side],
            device_id_type=MESH,
        )

    def send_parts(hh):
        for which in range(2):
            for side in range(2):
                part = (k_acc, v_acc)[which][hh, ROW * 3 * side : ROW * 3 * side + ROW, :]
                if which == 0:
                    part = part * SCALE
                part_out[hh, which, side] = part.astype(bf16)
                part_copy(hh, which, side).start()

    results = ((q_res, q_out), (k_res, k_out), (v_res, v_out))

    def send_result(hh, array):
        src, dst = results[array]
        into = dst.at[:, pl.ds(pl.multiple_of((me * MINE + hh) * D, D), D)]

        def rows(index):
            return src.at[hh, pl.ds(token_start(index), PIECE)]

        def send(step, carry):
            there = lax.rem(me + step, RING)
            pltpu.make_async_remote_copy(
                src_ref=rows(there),
                dst_ref=into,
                send_sem=out_send.at[hh, array],
                recv_sem=out_recv.at[array],
                device_id=ring_device(there),
                device_id_type=MESH,
            ).start()
            return carry

        lax.fori_loop(1, RING, send, 0)
        pltpu.make_async_copy(rows(me), into, out_recv.at[array]).start()

    def finish_head(hh):
        for which in range(2):
            for side in range(2):
                part_copy(hh, which, side).wait_recv()
                rows = ROW * (2 - side)
                total = (k_acc, v_acc)[which][hh, rows : rows + ROW, :]
                if which == 0:
                    total = total * SCALE
                total = total + part_in[hh, which, side].astype(f32)
                (k_res, v_res)[which][hh, rows - ROW : rows, :] = total.astype(bf16)
            send_result(hh, 1 + which)

    def attend(hh, row):
        queries = qb[hh, pl.ds(pl.multiple_of(row * ROW, ROW), ROW), :]
        grads = ob[hh, pl.ds(pl.multiple_of(row * ROW, ROW), ROW), :]
        listed = near[row, 0:1, :]
        bias = [
            jnp.where(listed[:, 1:2] >= 0, 0.0, ABSENT).astype(f32),
            None,
            jnp.where(listed[:, 7:8] >= 0, 0.0, ABSENT).astype(f32),
        ]
        chunks = 3 * ROW // CHUNK

        def keys_at(chunk):
            return pl.ds(pl.multiple_of(row * ROW + chunk * CHUNK, CHUNK), CHUNK)

        tops, sums, dots = [], [], []
        for chunk in range(chunks):
            scores = dot(kb[hh, keys_at(chunk), :], queries, 1, 1)
            dprobs = dot(vb[hh, keys_at(chunk), :], grads, 1, 1)
            top = jnp.max(scores, axis=0, keepdims=True)
            weights = jnp.exp2((scores - top) * (SCALE * LOG2E))
            sums.append(jnp.sum(weights, axis=0, keepdims=True))
            dots.append(jnp.sum(weights * dprobs, axis=0, keepdims=True))
            expon[chunk] = weights
            dprob[chunk] = dprobs
            shift = bias[chunk * CHUNK // ROW]
            tops.append(top if shift is None else top + shift)
        top = functools.reduce(jnp.maximum, tops)
        factors = [jnp.exp2((t - top) * (SCALE * LOG2E)) for t in tops]
        total = functools.reduce(jnp.add, [f * s for f, s in zip(factors, sums)])
        inverse = 1.0 / total
        row_dot = functools.reduce(jnp.add, [f * d for f, d in zip(factors, dots)]) * inverse
        query_grad = jnp.zeros((D, ROW), f32)
        for chunk in range(chunks):
            probs = expon[chunk] * (factors[chunk] * inverse)
            dscores = (probs * (dprob[chunk] - row_dot)).astype(bf16)
            v_acc[hh, keys_at(chunk), :] += dot(probs.astype(bf16), grads, 1, 0)
            k_acc[hh, keys_at(chunk), :] += dot(dscores, queries, 1, 0)
            query_grad += dot(kt[:, keys_at(chunk)], dscores, 1, 0)
        q_res[hh, pl.ds(pl.multiple_of(row * ROW, ROW), ROW), :] = (
            (query_grad * SCALE).T.astype(bf16)
        )

    send_inputs(0, (0, 1, 2, 3))
    near_copy = pltpu.make_async_remote_copy(
        src_ref=near_in,
        dst_ref=near.at[low],
        send_sem=near_sem.at[0],
        recv_sem=near_sem.at[1],
        device_id=partner,
        device_id_type=MESH,
    )
    near_copy.start()
    own_near = pltpu.make_async_copy(near_in, near.at[low], near_sem.at[2])
    own_near.start()
    send_inputs(1, (0, 1, 2, 3))
    send_inputs(2, (0, 1, 2, 3))
    k_acc[...] = jnp.zeros_like(k_acc)
    v_acc[...] = jnp.zeros_like(v_acc)
    wait_groups()
    send_halo(0)
    near_copy.wait()
    own_near.wait()

    def step(index, carry):
        hh, row = index // 2, index % 2

        @pl.when(row == 0)
        def _():
            wait_head(hh)
            kt[...] = kb[hh].T

        attend(hh, row)

        @pl.when(row == 1)
        def _():
            send_parts(hh)
            send_result(hh, 0)

        @pl.when(index == 0)
        def _():
            send_halo(1)

        @pl.when(index == 2)
        def _():
            send_halo(2)
            finish_head(0)

        @pl.when(index == 4)
        def _():
            finish_head(1)

        return carry

    lax.fori_loop(0, 2 * MINE, step, 0)
    finish_head(MINE - 1)

    def drain(hh, carry):
        wait_inputs_sent(hh, (0, 1, 2, 3))
        for which in range(2):
            for side in range(2):
                halo_copy(hh, which, side).wait_send()
                part_copy(hh, which, side).wait_send()
        for array in range(3):
            wait_bytes(kb.at[0, pl.ds(0, (RING - 1) * PIECE)], out_send.at[hh, array])
        return carry

    lax.fori_loop(0, MINE, drain, 0)
    for array in range(3):
        wait_bytes(results[array][1], out_recv.at[array])


def per_device(queries, keys, values, grad_out, neighbours):
    vmem, sem = pltpu.VMEM, pltpu.SemaphoreType.DMA
    out = pltpu.VMEM(queries.shape, bf16)
    anywhere = pl.BlockSpec(memory_space=pl.ANY)
    chunks = 3 * ROW // CHUNK
    return pl.pallas_call(
        kernel,
        out_shape=(out, out, out),
        in_specs=[anywhere] * 5,
        out_specs=(pl.BlockSpec(memory_space=vmem),) * 3,
        scratch_shapes=[
            vmem((MINE, 4 * ROW, D), bf16),
            vmem((MINE, 4 * ROW, D), bf16),
            vmem((MINE, 2 * ROW, D), bf16),
            vmem((MINE, 2 * ROW, D), bf16),
            vmem((2,) + neighbours.shape, jnp.int32),
            vmem((D, 4 * ROW), bf16),
            vmem((chunks, CHUNK, ROW), f32),
            vmem((chunks, CHUNK, ROW), f32),
            vmem((MINE, 4 * ROW, D), f32),
            vmem((MINE, 4 * ROW, D), f32),
            vmem((MINE, 2, 2, ROW, D), bf16),
            vmem((MINE, 2, 2, ROW, D), bf16),
            vmem((MINE, 2 * ROW, D), bf16),
            vmem((MINE, 2 * ROW, D), bf16),
            vmem((MINE, 2 * ROW, D), bf16),
            sem((3,)),
            sem((MINE, 6)),
            sem((MINE, 4)),
            sem((MINE, 4)),
            sem((MINE, 4)),
            sem((MINE, 4)),
            sem((MINE, 4)),
            sem((3,)),
            sem((MINE, 3)),
            pltpu.SemaphoreType.REGULAR,
        ],
        compiler_params=pltpu.CompilerParams(
            collective_id=0, has_side_effects=True, vmem_limit_bytes=52 << 20
        ),
        cost_estimate=pl.CostEstimate(
            flops=13_600_000_000, bytes_accessed=16_000_000, transcendentals=10_600_000
        ),
    )(queries, keys, values, grad_out, neighbours)


def solution(mesh):
    tokens = P(("frame", "head"), None)
    return jax.shard_map(
        per_device,
        mesh=mesh,
        in_specs=(tokens, tokens, tokens, tokens, P("frame", None)),
        out_specs=(tokens, tokens, tokens),
        check_vma=False,
    )
```

```python
import functools

import jax
import jax.numpy as jnp
from jax import lax
from jax.experimental import pallas as pl
from jax.experimental.pallas import tpu as pltpu
from jax.sharding import PartitionSpec as P

D = 128
TILE = 384
ROW = 2 * TILE
PIECE = TILE // 2
STEPS = 6
RING = 4
SCALE = D**-0.5
LOG2E = 1.4426950408889634
ABSENT = -1e30
f32 = jnp.float32
bf16 = jnp.bfloat16
MESH = pl.DeviceIdType.MESH


def dot(a, b, dim_a, dim_b):
    return lax.dot_general(a, b, (((dim_a,), (dim_b,)), ((), ())), preferred_element_type=f32)


def wait_bytes(ref, sem):
    pltpu.make_async_copy(ref, ref, sem).wait()


def remote(src, dst, send_sem, recv_sem, device):
    return pltpu.make_async_remote_copy(
        src_ref=src, dst_ref=dst, send_sem=send_sem, recv_sem=recv_sem, device_id=device,
        device_id_type=MESH,
    )


def rows_at(start, size):
    return pl.ds(pl.multiple_of(start, PIECE), size)


def kernel(
    q_in, k_in, v_in, o_in, near_in,
    q_out, k_out, v_out,
    kb, vb, qb, ob, near, kt, expon, dprob, tops, k_acc, v_acc,
    stat_out, stat_in, part_out, part_in, q_acc, q_keep, q_part, q_other, q_res, k_res, v_res,
    near_sem, in_recv, in_send, fwd_send, halo_recv, halo_send, stat_sem,
    part_recv, part_send, q_sem, out_recv, out_send, entered,
):
    frame, head = lax.axis_index("frame"), lax.axis_index("head")
    group, low = frame // 2, frame % 2
    groups = lax.axis_size("frame") // 2
    x, core = (head // 2) * 2 + low, head % 2
    peer = 1 - core

    def device(chip, which_core):
        return (group * 2 + chip % 2, (chip // 2) * 2 + which_core)

    def places(n):
        parity = (x + n) % 2
        partner = (x + 5 - 2 * parity) % RING
        outer = (x + 3 + 2 * parity) % RING
        mine = (x + RING - parity) % RING
        theirs = (outer + RING - 1 + parity) % RING
        return partner, outer, mine, theirs

    def columns(pair, which_core, n):
        return pl.ds(pl.multiple_of((pair * STEPS + which_core * 3 + n // 2) * D, D), D)

    def tile_slot(chip):
        return (chip % 2) * 2 + chip // 2

    prev_device = (lax.rem(group + groups - 1, groups) * 2 + low, head)
    next_device = (lax.rem(group + 1, groups) * 2 + low, head)
    after, before = (x + 1) % RING, (x + 3) % RING

    barrier = pltpu.get_barrier_semaphore()
    other = device(x, peer)
    for chip in (after, before):
        pl.semaphore_signal(barrier, inc=1, device_id=device(chip, 0), device_id_type=MESH)
    for there in (prev_device, next_device):
        pl.semaphore_signal(
            barrier, inc=1, device_id=(there[0], head + 1 - core), device_id_type=MESH
        )

    @pl.when(core == 0)
    def _():
        pl.semaphore_signal(barrier, inc=1, device_id=other, device_id_type=MESH)
        pl.semaphore_wait(barrier, 5)
        pl.semaphore_signal(entered, inc=1, device_id=other, device_id_type=MESH)

    @pl.when(core == 1)
    def _():
        pl.semaphore_signal(barrier, inc=1, device_id=other, device_id_type=MESH)
        pl.semaphore_wait(entered, 1)

    def wait_groups():
        @pl.when(core == 1)
        def _():
            pl.semaphore_wait(barrier, 5)
            pl.semaphore_signal(entered, inc=1, device_id=other, device_id_type=MESH)

        @pl.when(core == 0)
        def _():
            pl.semaphore_wait(entered, 1)

    key_start = (1 + low) * TILE + core * PIECE
    query_start = tile_slot(x) * TILE + core * PIECE
    inputs = ((k_in, kb, key_start), (v_in, vb, key_start), (q_in, qb, query_start), (o_in, ob, query_start))

    def far_inputs(n, arrays):
        _, outer, _, theirs = places(n)
        for array in arrays:
            src, dst, start = inputs[array]
            got = in_recv.at[n, 2 * array + low if array < 2 else 2 + array]
            for c in range(2):
                remote(
                    src.at[:, columns(theirs, c, n)],
                    dst.at[n, rows_at(start, PIECE)],
                    in_send.at[n, array],
                    got,
                    device(outer, c),
                ).start()

    def near_inputs(n, arrays):
        partner, _, mine, _ = places(n)
        for array in arrays:
            src, dst, start = inputs[array]
            into, sent = dst.at[n, rows_at(start, PIECE)], in_send.at[n, array]
            got = in_recv.at[n, 2 * array + low if array < 2 else 4 + array]
            if array >= 2:
                for c in range(2):
                    remote(
                        src.at[:, columns(mine, c, n)], into, sent, got, device(partner, c)
                    ).start()
            remote(src.at[:, columns(mine, peer, n)], into, sent, got, device(x, peer)).start()
            pltpu.make_async_copy(src.at[:, columns(mine, core, n)], into, got).start()

    def forward_copy(n, which):
        partner, outer, _, _ = places(n)
        there = (qb, ob)[which].at[n, rows_at(tile_slot(outer) * TILE, TILE)]
        return there, remote(
            there, there, fwd_send.at[n, which], in_recv.at[n, 6 + which], device(partner, core)
        )

    def forward(n):
        for which in range(2):
            tile, copy = forward_copy(n, which)
            wait_bytes(tile, in_recv.at[n, 4 + which])
            copy.start()

    def halo_copy(n, which, side):
        buffer = (kb, vb)[which]
        return remote(
            buffer.at[n, pl.ds(TILE * (1 + side), TILE)],
            buffer.at[n, pl.ds(TILE * 3 * (1 - side), TILE)],
            halo_send.at[n, 2 * which + side],
            halo_recv.at[n, 2 * which + side],
            (prev_device, next_device)[side],
        )

    def send_halo(n):
        for which in range(2):
            for side in range(2):
                wait_bytes(
                    (kb, vb)[which].at[n, pl.ds(TILE * (1 + side), TILE)],
                    in_recv.at[n, 2 * which + side],
                )
                halo_copy(n, which, side).start()

    def wait_step(n):
        for which in range(2):
            wait_bytes((qb, ob)[which].at[n, pl.ds(0, 3 * TILE)], in_recv.at[n, 6 + which])
        for which in range(2):
            for side in range(2):
                halo_copy(n, which, side).wait_recv()

    def stat_copy(n, row):
        partner, _, _, _ = places(n)
        return remote(
            stat_out.at[n, row], stat_in.at[n, row], stat_sem.at[0, n, row], stat_sem.at[1, n, row],
            device(partner, core),
        )

    def query_copy(n):
        partner, _, _, _ = places(n)
        return remote(
            q_part.at[n], q_other.at[n], q_sem.at[0, n], q_sem.at[1, n], device(partner, core)
        )

    def part_copy(n, which, side):
        return remote(
            part_out.at[n, which, side],
            part_in.at[n, which, side],
            part_send.at[n, 2 * which + side],
            part_recv.at[n, 2 * which + side],
            (prev_device, next_device)[side],
        )

    def send_parts(n):
        for which in range(2):
            for side in range(2):
                part = (k_acc, v_acc)[which][n, TILE * 3 * side : TILE * 3 * side + TILE, :]
                if which == 0:
                    part = part * SCALE
                part_out[n, which, side] = part.astype(bf16)
                part_copy(n, which, side).start()

    results = ((q_res, q_out), (k_res, k_out), (v_res, v_out))

    def send_result(n, array):
        _, outer, mine, _ = places(n)
        src, dst = results[array]
        into = dst.at[:, columns(mine, core, n)]
        sent, got = out_send.at[n, array], out_recv.at[array]
        for c in range(2):
            remote(
                src.at[n, 1 - low, pl.ds(c * PIECE, PIECE)], into, sent, got, device(outer, c)
            ).start()
        remote(
            src.at[n, low, rows_at(peer * PIECE, PIECE)], into, sent, got, device(x, peer)
        ).start()
        pltpu.make_async_copy(src.at[n, low, rows_at(core * PIECE, PIECE)], into, got).start()

    def finish_queries(n):
        query_copy(n).wait_recv()
        for row in range(2):
            q_res[n, row] = (q_keep[n, row] + q_other[n, row].astype(f32)).astype(bf16)
        send_result(n, 0)

    def finish_keys(n):
        for which in range(2):
            for side in range(2):
                part_copy(n, which, side).wait_recv()
                slot = 2 - side
                total = (k_acc, v_acc)[which][n, TILE * slot : TILE * slot + TILE, :]
                if which == 0:
                    total = total * SCALE
                total = total + part_in[n, which, side].astype(f32)
                (k_res, v_res)[which][n, slot - 1] = total.astype(bf16)
            send_result(n, 1 + which)

    def keys_at(row, slot):
        return pl.ds(pl.multiple_of((row + slot) * TILE, TILE), TILE)

    def first_half(n, row):
        queries = qb[n, rows_at(row * ROW, ROW), :]
        grads = ob[n, rows_at(row * ROW, ROW), :]
        listed = near[row, 0:1, :]
        bias = [
            jnp.where(listed[:, 1:2] >= 0, 0.0, ABSENT).astype(f32),
            None,
            jnp.where(listed[:, 7:8] >= 0, 0.0, ABSENT).astype(f32),
        ]
        peaks, sums, dots = [], [], []
        for slot in range(3):
            scores = dot(kb[n, keys_at(row, slot), :], queries, 1, 1)
            dprobs = dot(vb[n, keys_at(row, slot), :], grads, 1, 1)
            peak = jnp.max(scores, axis=0, keepdims=True)
            weights = jnp.exp2((scores - peak) * (SCALE * LOG2E))
            sums.append(jnp.sum(weights, axis=0, keepdims=True))
            dots.append(jnp.sum(weights * dprobs, axis=0, keepdims=True))
            expon[row, slot] = weights
            dprob[row, slot] = dprobs
            if bias[slot] is not None:
                peak = peak + bias[slot]
            tops[row, slot : slot + 1, :] = peak
            peaks.append(peak)
        top = functools.reduce(jnp.maximum, peaks)
        factors = [jnp.exp2((peak - top) * (SCALE * LOG2E)) for peak in peaks]
        stat_out[n, row, 0:1, :] = top
        stat_out[n, row, 1:2, :] = functools.reduce(jnp.add, [f * s for f, s in zip(factors, sums)])
        stat_out[n, row, 2:3, :] = functools.reduce(jnp.add, [f * s for f, s in zip(factors, dots)])

    def second_half(n, row):
        queries = qb[n, rows_at(row * ROW, ROW), :]
        grads = ob[n, rows_at(row * ROW, ROW), :]
        here, there = stat_out[n, row], stat_in[n, row]
        top = jnp.maximum(here[0:1], there[0:1])
        factor_here = jnp.exp2((here[0:1] - top) * (SCALE * LOG2E))
        factor_there = jnp.exp2((there[0:1] - top) * (SCALE * LOG2E))
        inverse = 1.0 / (factor_here * here[1:2] + factor_there * there[1:2])
        row_dot = (factor_here * here[2:3] + factor_there * there[2:3]) * inverse
        query_grad = jnp.zeros((D, ROW), f32)
        for slot in range(3):
            factor = jnp.exp2((tops[row, slot : slot + 1, :] - top) * (SCALE * LOG2E)) * inverse
            probs = expon[row, slot] * factor
            dscores = (probs * (dprob[row, slot] - row_dot)).astype(bf16)
            v_acc[n, keys_at(row, slot), :] += dot(probs.astype(bf16), grads, 1, 0)
            k_acc[n, keys_at(row, slot), :] += dot(dscores, queries, 1, 0)
            query_grad += dot(kt[:, keys_at(row, slot)], dscores, 1, 0)
        q_acc[...] = (query_grad * SCALE).T
        _, outer, _, _ = places(n)
        column = jnp.where(row == low, x // 2, outer // 2)
        q_keep[n, row] = q_acc[rows_at(column * TILE, TILE), :]
        q_part[n, row] = q_acc[rows_at((1 - column) * TILE, TILE), :].astype(bf16)

    near_copy = remote(near_in, near.at[low], near_sem.at[0], near_sem.at[1], device(after, core))
    own_near = pltpu.make_async_copy(near_in, near.at[low], near_sem.at[2])

    keys_values, queries_grads = (0, 1), (2, 3)
    far_inputs(1, (3,))
    far_inputs(0, (2,))
    near_copy.start()
    own_near.start()
    near_inputs(3, keys_values)
    near_inputs(0, keys_values)
    far_inputs(1, keys_values)
    near_inputs(0, queries_grads)
    far_inputs(0, keys_values)
    far_inputs(2, (3,))
    far_inputs(0, (3,))
    near_inputs(2, keys_values)
    k_acc[...] = jnp.zeros_like(k_acc)
    v_acc[...] = jnp.zeros_like(v_acc)
    far_inputs(2, keys_values)
    far_inputs(2, (2,))
    near_inputs(1, queries_grads)
    near_inputs(4, keys_values)
    wait_groups()
    send_halo(0)
    far_inputs(1, (2,))
    forward(0)
    far_inputs(3, keys_values)
    near_inputs(1, keys_values)
    send_halo(1)
    send_halo(2)
    forward(1)
    near_copy.wait()
    own_near.wait()

    def step(n, carry):
        wait_step(n)
        kt[...] = kb[n].T

        def first(row, inner):
            first_half(n, row)
            stat_copy(n, row).start()
            return inner

        lax.fori_loop(0, 2, first, 0)
        @pl.when(n == 0)
        def _():
            far_inputs(4, (3,))
            far_inputs(3, (2,))
            far_inputs(4, (2,))
            far_inputs(3, (3,))
            forward(2)
            near_inputs(2, queries_grads)
            near_inputs(4, queries_grads)

        @pl.when(n == 1)
        def _():
            send_halo(3)
            far_inputs(4, keys_values)
            near_inputs(3, queries_grads)
            forward(3)

        @pl.when(n == 2)
        def _():
            far_inputs(5, (2,))
            near_inputs(5, keys_values)
            far_inputs(5, keys_values)
            send_halo(4)
            forward(4)
            far_inputs(5, (3,))
            query_copy(1).start()

        @pl.when(n == 3)
        def _():
            finish_keys(0)
            send_halo(5)
            query_copy(2).start()
            near_inputs(5, queries_grads)

        @pl.when(n == 4)
        def _():
            query_copy(3).start()
            finish_keys(1)
            query_copy(0).start()

        @pl.when(n == 5)
        def _():
            query_copy(4).start()
            finish_keys(2)
            finish_queries(1)
            finish_queries(2)

        def second(row, inner):
            stat_copy(n, row).wait_recv()
            second_half(n, row)
            return inner

        lax.fori_loop(0, 2, second, 0)
        send_parts(n)
        @pl.when(n == 3)
        def _():
            forward(5)

        @pl.when(n == 5)
        def _():
            query_copy(5).start()
            finish_queries(3)

        return carry

    lax.fori_loop(0, STEPS, step, 0)
    finish_keys(4)
    finish_keys(3)
    finish_keys(5)
    finish_queries(0)
    finish_queries(5)
    finish_queries(4)

    def drain(n, carry):
        for array in range(4):
            wait_bytes(qb.at[0, pl.ds(0, (3 if array < 2 else 5) * PIECE)], in_send.at[n, array])
        for which in range(2):
            forward_copy(n, which)[1].wait_send()
            for side in range(2):
                halo_copy(n, which, side).wait_send()
                part_copy(n, which, side).wait_send()
        for row in range(2):
            stat_copy(n, row).wait_send()
        query_copy(n).wait_send()
        for array in range(3):
            wait_bytes(qb.at[0, pl.ds(0, 3 * PIECE)], out_send.at[n, array])
        return carry

    lax.fori_loop(0, STEPS, drain, 0)
    for array in range(3):
        wait_bytes(results[array][1], out_recv.at[array])


def per_device(queries, keys, values, grad_out, neighbours):
    vmem, sem = pltpu.VMEM, pltpu.SemaphoreType.DMA
    out = vmem(queries.shape, bf16)
    anywhere = pl.BlockSpec(memory_space=pl.ANY)
    tokens, result = vmem((STEPS, 4 * TILE, D), bf16), vmem((STEPS, 2, TILE, D), bf16)
    scores, sums = vmem((2, 3, TILE, ROW), f32), vmem((STEPS, 4 * TILE, D), f32)
    stats, parts = vmem((STEPS, 2, 3, ROW), f32), vmem((STEPS, 2, 2, TILE, D), bf16)
    return pl.pallas_call(
        kernel,
        out_shape=(out, out, out),
        in_specs=[anywhere] * 5,
        out_specs=(pl.BlockSpec(memory_space=vmem),) * 3,
        scratch_shapes=[
            tokens, tokens, tokens, tokens,
            vmem((2,) + neighbours.shape, jnp.int32),
            vmem((D, 4 * TILE), bf16),
            scores, scores,
            vmem((2, 3, ROW), f32),
            sums, sums,
            stats, stats,
            parts, parts,
            vmem((ROW, D), f32),
            vmem((STEPS, 2, TILE, D), f32),
            result, result,
            result, result, result,
            sem((3,)),
            sem((STEPS, 8)),
            sem((STEPS, 4)),
            sem((STEPS, 2)),
            sem((STEPS, 4)),
            sem((STEPS, 4)),
            sem((2, STEPS, 2)),
            sem((STEPS, 4)),
            sem((STEPS, 4)),
            sem((2, STEPS)),
            sem((3,)),
            sem((STEPS, 3)),
            pltpu.SemaphoreType.REGULAR,
        ],
        compiler_params=pltpu.CompilerParams(
            collective_id=0, has_side_effects=True, vmem_limit_bytes=56 << 20
        ),
        cost_estimate=pl.CostEstimate(
            flops=13_600_000_000, bytes_accessed=16_000_000, transcendentals=10_600_000
        ),
    )(queries, keys, values, grad_out, neighbours)


def solution(mesh):
    tokens = P(("frame", "head"), None)
    return jax.shard_map(
        per_device,
        mesh=mesh,
        in_specs=(tokens, tokens, tokens, tokens, P("frame", None)),
        out_specs=(tokens, tokens, tokens),
        check_vma=False,
    )
```

```python
import functools

import jax
import jax.numpy as jnp
from jax import lax
from jax.experimental import pallas as pl
from jax.experimental.pallas import tpu as pltpu
from jax.sharding import PartitionSpec as P

D = 128
TILE = 384
ROW = 2 * TILE
PIECE = TILE // 2
STEPS = 6
RING = 4
SCALE = D**-0.5
LOG2E = 1.4426950408889634
ABSENT = -1e30
f32 = jnp.float32
bf16 = jnp.bfloat16
MESH = pl.DeviceIdType.MESH


def dot(a, b, dim_a, dim_b):
    return lax.dot_general(a, b, (((dim_a,), (dim_b,)), ((), ())), preferred_element_type=f32)


def wait_bytes(ref, sem):
    pltpu.make_async_copy(ref, ref, sem).wait()


def remote(src, dst, send_sem, recv_sem, device):
    return pltpu.make_async_remote_copy(
        src_ref=src, dst_ref=dst, send_sem=send_sem, recv_sem=recv_sem, device_id=device,
        device_id_type=MESH,
    )


def rows_at(start, size):
    return pl.ds(pl.multiple_of(start, PIECE), size)


def kernel(
    q_in, k_in, v_in, o_in, near_in,
    q_out, k_out, v_out,
    kb, vb, qb, ob, near, kt, expon, dprob, tops, k_acc, v_acc,
    stat_out, stat_in, part_out, part_in, q_acc, q_keep, q_part, q_other, q_res, k_res, v_res,
    near_sem, in_recv, in_send, fwd_send, halo_recv, halo_send, stat_sem,
    part_recv, part_send, q_sem, out_recv, out_send, entered,
):
    frame, head = lax.axis_index("frame"), lax.axis_index("head")
    group, low = frame // 2, frame % 2
    groups = lax.axis_size("frame") // 2
    x, core = (head // 2) * 2 + low, head % 2
    peer = 1 - core

    def device(chip, which_core):
        return (group * 2 + chip % 2, (chip // 2) * 2 + which_core)

    def places(n):
        parity = (x + n) % 2
        partner = (x + 5 - 2 * parity) % RING
        outer = (x + 3 + 2 * parity) % RING
        mine = (x + RING - parity) % RING
        theirs = (outer + RING - 1 + parity) % RING
        return partner, outer, mine, theirs

    def columns(pair, which_core, n):
        return pl.ds(pl.multiple_of((pair * STEPS + which_core * 3 + n // 2) * D, D), D)

    def tile_slot(chip):
        return (chip % 2) * 2 + chip // 2

    prev_device = (lax.rem(group + groups - 1, groups) * 2 + low, head)
    next_device = (lax.rem(group + 1, groups) * 2 + low, head)
    after, before = (x + 1) % RING, (x + 3) % RING

    barrier = pltpu.get_barrier_semaphore()
    other = device(x, peer)
    for chip in (after, before):
        pl.semaphore_signal(barrier, inc=1, device_id=device(chip, 0), device_id_type=MESH)
    for there in (prev_device, next_device):
        pl.semaphore_signal(
            barrier, inc=1, device_id=(there[0], head + 1 - core), device_id_type=MESH
        )

    @pl.when(core == 0)
    def _():
        pl.semaphore_signal(barrier, inc=1, device_id=other, device_id_type=MESH)
        pl.semaphore_wait(barrier, 5)
        pl.semaphore_signal(entered, inc=1, device_id=other, device_id_type=MESH)

    @pl.when(core == 1)
    def _():
        pl.semaphore_signal(barrier, inc=1, device_id=other, device_id_type=MESH)
        pl.semaphore_wait(entered, 1)

    def wait_groups():
        @pl.when(core == 1)
        def _():
            pl.semaphore_wait(barrier, 5)
            pl.semaphore_signal(entered, inc=1, device_id=other, device_id_type=MESH)

        @pl.when(core == 0)
        def _():
            pl.semaphore_wait(entered, 1)

    key_start = (1 + low) * TILE + core * PIECE
    query_start = tile_slot(x) * TILE + core * PIECE
    inputs = ((k_in, kb, key_start), (v_in, vb, key_start), (q_in, qb, query_start), (o_in, ob, query_start))

    def far_inputs(n, array):
        _, outer, _, theirs = places(n)
        src, dst, start = inputs[array]
        got = in_recv.at[n, 2 * array + low if array < 2 else 2 + array]
        for c in range(2):
            remote(
                src.at[:, columns(theirs, c, n)],
                dst.at[n, rows_at(start, PIECE)],
                in_send.at[n, array],
                got,
                device(outer, c),
            ).start()

    def near_inputs(n, array):
        partner, _, mine, _ = places(n)
        src, dst, start = inputs[array]
        into, sent = dst.at[n, rows_at(start, PIECE)], in_send.at[n, array]
        got = in_recv.at[n, 2 * array + low if array < 2 else 4 + array]
        if array >= 2:
            for c in range(2):
                remote(src.at[:, columns(mine, c, n)], into, sent, got, device(partner, c)).start()
        remote(src.at[:, columns(mine, peer, n)], into, sent, got, device(x, peer)).start()
        pltpu.make_async_copy(src.at[:, columns(mine, core, n)], into, got).start()

    def forward_copy(n, which):
        partner, outer, _, _ = places(n)
        there = (qb, ob)[which].at[n, rows_at(tile_slot(outer) * TILE, TILE)]
        return there, remote(
            there, there, fwd_send.at[n, which], in_recv.at[n, 6 + which], device(partner, core)
        )

    def forward(n, which):
        tile, copy = forward_copy(n, which)
        wait_bytes(tile, in_recv.at[n, 4 + which])
        copy.start()

    def halo_copy(n, which, side):
        buffer = (kb, vb)[which]
        return remote(
            buffer.at[n, pl.ds(TILE * (1 + side), TILE)],
            buffer.at[n, pl.ds(TILE * 3 * (1 - side), TILE)],
            halo_send.at[n, 2 * which + side],
            halo_recv.at[n, 2 * which + side],
            (prev_device, next_device)[side],
        )

    def send_halo(n, which):
        for side in range(2):
            wait_bytes(
                (kb, vb)[which].at[n, pl.ds(TILE * (1 + side), TILE)],
                in_recv.at[n, 2 * which + side],
            )
            halo_copy(n, which, side).start()

    def wait_step(n):
        for which in range(2):
            wait_bytes((qb, ob)[which].at[n, pl.ds(0, 3 * TILE)], in_recv.at[n, 6 + which])
        for which in range(2):
            for side in range(2):
                halo_copy(n, which, side).wait_recv()

    def stat_copy(n, row):
        partner, _, _, _ = places(n)
        return remote(
            stat_out.at[n, row], stat_in.at[n, row], stat_sem.at[0, n, row], stat_sem.at[1, n, row],
            device(partner, core),
        )

    def query_copy(n):
        partner, _, _, _ = places(n)
        return remote(
            q_part.at[n], q_other.at[n], q_sem.at[0, n], q_sem.at[1, n], device(partner, core)
        )

    def part_copy(n, which, side):
        return remote(
            part_out.at[n, which, side],
            part_in.at[n, which, side],
            part_send.at[n, 2 * which + side],
            part_recv.at[n, 2 * which + side],
            (prev_device, next_device)[side],
        )

    def send_parts(n):
        for which in range(2):
            for side in range(2):
                part = (k_acc, v_acc)[which][n, TILE * 3 * side : TILE * 3 * side + TILE, :]
                if which == 0:
                    part = part * SCALE
                part_out[n, which, side] = part.astype(bf16)
                part_copy(n, which, side).start()

    results = ((q_res, q_out), (k_res, k_out), (v_res, v_out))

    def send_result(n, array):
        _, outer, mine, _ = places(n)
        src, dst = results[array]
        into = dst.at[:, columns(mine, core, n)]
        sent, got = out_send.at[n, array], out_recv.at[array]
        for c in range(2):
            remote(
                src.at[n, 1 - low, pl.ds(c * PIECE, PIECE)], into, sent, got, device(outer, c)
            ).start()
        remote(
            src.at[n, low, rows_at(peer * PIECE, PIECE)], into, sent, got, device(x, peer)
        ).start()
        pltpu.make_async_copy(src.at[n, low, rows_at(core * PIECE, PIECE)], into, got).start()

    def finish_queries(n):
        query_copy(n).wait_recv()
        for row in range(2):
            q_res[n, row] = (q_keep[n, row] + q_other[n, row].astype(f32)).astype(bf16)
        send_result(n, 0)

    def finish_keys(n, which):
        for side in range(2):
            part_copy(n, which, side).wait_recv()
            slot = 2 - side
            total = (k_acc, v_acc)[which][n, TILE * slot : TILE * slot + TILE, :]
            if which == 0:
                total = total * SCALE
            total = total + part_in[n, which, side].astype(f32)
            (k_res, v_res)[which][n, slot - 1] = total.astype(bf16)
        send_result(n, 1 + which)

    def keys_at(row, slot):
        return pl.ds(pl.multiple_of((row + slot) * TILE, TILE), TILE)

    def first_half(n, row):
        queries = qb[n, rows_at(row * ROW, ROW), :]
        grads = ob[n, rows_at(row * ROW, ROW), :]
        listed = near[row, 0:1, :]
        bias = [
            jnp.where(listed[:, 1:2] >= 0, 0.0, ABSENT).astype(f32),
            None,
            jnp.where(listed[:, 7:8] >= 0, 0.0, ABSENT).astype(f32),
        ]
        peaks, sums, dots = [], [], []
        for slot in range(3):
            scores = dot(kb[n, keys_at(row, slot), :], queries, 1, 1)
            dprobs = dot(vb[n, keys_at(row, slot), :], grads, 1, 1)
            peak = jnp.max(scores, axis=0, keepdims=True)
            weights = jnp.exp2((scores - peak) * (SCALE * LOG2E))
            sums.append(jnp.sum(weights, axis=0, keepdims=True))
            dots.append(jnp.sum(weights * dprobs, axis=0, keepdims=True))
            expon[row, slot] = weights
            dprob[row, slot] = dprobs
            if bias[slot] is not None:
                peak = peak + bias[slot]
            tops[row, slot : slot + 1, :] = peak
            peaks.append(peak)
        top = functools.reduce(jnp.maximum, peaks)
        factors = [jnp.exp2((peak - top) * (SCALE * LOG2E)) for peak in peaks]
        stat_out[n, row, 0:1, :] = top
        stat_out[n, row, 1:2, :] = functools.reduce(jnp.add, [f * s for f, s in zip(factors, sums)])
        stat_out[n, row, 2:3, :] = functools.reduce(jnp.add, [f * s for f, s in zip(factors, dots)])

    def second_half(n, row):
        queries = qb[n, rows_at(row * ROW, ROW), :]
        grads = ob[n, rows_at(row * ROW, ROW), :]
        here, there = stat_out[n, row], stat_in[n, row]
        top = jnp.maximum(here[0:1], there[0:1])
        factor_here = jnp.exp2((here[0:1] - top) * (SCALE * LOG2E))
        factor_there = jnp.exp2((there[0:1] - top) * (SCALE * LOG2E))
        inverse = 1.0 / (factor_here * here[1:2] + factor_there * there[1:2])
        row_dot = (factor_here * here[2:3] + factor_there * there[2:3]) * inverse
        query_grad = jnp.zeros((D, ROW), f32)
        for slot in range(3):
            factor = jnp.exp2((tops[row, slot : slot + 1, :] - top) * (SCALE * LOG2E)) * inverse
            probs = expon[row, slot] * factor
            dscores = (probs * (dprob[row, slot] - row_dot)).astype(bf16)
            v_acc[n, keys_at(row, slot), :] += dot(probs.astype(bf16), grads, 1, 0)
            k_acc[n, keys_at(row, slot), :] += dot(dscores, queries, 1, 0)
            query_grad += dot(kt[:, keys_at(row, slot)], dscores, 1, 0)
        q_acc[...] = (query_grad * SCALE).T
        _, outer, _, _ = places(n)
        column = jnp.where(row == low, x // 2, outer // 2)
        q_keep[n, row] = q_acc[rows_at(column * TILE, TILE), :]
        q_part[n, row] = q_acc[rows_at((1 - column) * TILE, TILE), :].astype(bf16)

    near_copy = remote(near_in, near.at[low], near_sem.at[0], near_sem.at[1], device(after, core))
    own_near = pltpu.make_async_copy(near_in, near.at[low], near_sem.at[2])

    far_inputs(0, 0)
    far_inputs(1, 2)
    near_copy.start()
    own_near.start()
    far_inputs(1, 0)
    far_inputs(1, 3)
    far_inputs(1, 1)
    near_inputs(0, 1)
    near_inputs(4, 1)
    far_inputs(0, 1)
    far_inputs(0, 3)
    near_inputs(0, 2)
    near_inputs(0, 0)
    far_inputs(2, 3)
    k_acc[...] = jnp.zeros_like(k_acc)
    v_acc[...] = jnp.zeros_like(v_acc)
    wait_groups()
    send_halo(0, 1)
    far_inputs(2, 0)
    near_inputs(5, 0)
    near_inputs(5, 1)
    far_inputs(0, 2)
    near_inputs(0, 3)
    far_inputs(2, 1)
    send_halo(0, 0)
    forward(1, 0)
    near_inputs(1, 2)
    near_inputs(1, 3)
    near_inputs(1, 0)
    send_halo(1, 0)
    near_inputs(2, 1)
    forward(0, 1)
    far_inputs(2, 2)
    near_inputs(1, 1)
    forward(1, 1)
    near_inputs(2, 0)
    far_inputs(4, 2)
    far_inputs(4, 1)
    forward(0, 0)
    near_inputs(2, 3)
    send_halo(1, 1)
    near_inputs(3, 0)
    near_inputs(5, 3)
    near_inputs(2, 2)
    send_halo(2, 0)
    near_copy.wait()
    own_near.wait()

    def step(n, carry):
        wait_step(n)
        kt[...] = kb[n].T

        def first(row, inner):
            first_half(n, row)
            stat_copy(n, row).start()

            @pl.when(jnp.logical_and(n == 1, row == 0))
            def _():
                forward(2, 0)
                far_inputs(3, 3)

            return inner

        lax.fori_loop(0, 2, first, 0)

        @pl.when(n == 0)
        def _():
            far_inputs(3, 0)
            far_inputs(3, 2)
            far_inputs(3, 1)
            near_inputs(3, 1)
            near_inputs(4, 0)

        @pl.when(n == 1)
        def _():
            near_inputs(3, 3)
            send_halo(3, 0)
            far_inputs(5, 0)
            far_inputs(5, 3)
            far_inputs(4, 0)
            send_halo(4, 1)
            near_inputs(3, 2)
            send_halo(3, 1)
            near_inputs(5, 2)
            forward(3, 0)

        @pl.when(n == 2)
        def _():
            far_inputs(5, 1)
            forward(4, 0)
            send_halo(4, 0)
            far_inputs(5, 2)
            near_inputs(4, 3)
            forward(3, 1)
            far_inputs(4, 3)
            near_inputs(4, 2)
            forward(5, 1)

        @pl.when(n == 3)
        def _():
            send_halo(5, 0)
            query_copy(1).start()
            forward(4, 1)
            finish_keys(0, 1)
            query_copy(2).start()
            send_halo(5, 1)
            finish_keys(0, 0)
            forward(5, 0)

        @pl.when(n == 4)
        def _():
            query_copy(0).start()
            finish_keys(2, 1)
            finish_keys(1, 1)
            finish_queries(1)
            finish_keys(1, 0)

        @pl.when(n == 5)
        def _():
            finish_keys(3, 1)
            finish_queries(2)
            query_copy(4).start()
            finish_keys(2, 0)

        def second(row, inner):
            stat_copy(n, row).wait_recv()
            second_half(n, row)

            @pl.when(jnp.logical_and(n == 0, row == 0))
            def _():
                forward(2, 1)
                send_halo(2, 1)

            return inner

        lax.fori_loop(0, 2, second, 0)
        send_parts(n)

        @pl.when(n == 3)
        def _():
            query_copy(3).start()

        return carry

    lax.fori_loop(0, STEPS, step, 0)
    query_copy(5).start()
    finish_keys(4, 0)
    finish_keys(4, 1)
    finish_keys(3, 0)
    finish_queries(3)
    finish_queries(4)
    finish_queries(5)
    finish_keys(5, 0)
    finish_queries(0)
    finish_keys(5, 1)

    def drain(n, carry):
        for array in range(4):
            wait_bytes(qb.at[0, pl.ds(0, (3 if array < 2 else 5) * PIECE)], in_send.at[n, array])
        for which in range(2):
            forward_copy(n, which)[1].wait_send()
            for side in range(2):
                halo_copy(n, which, side).wait_send()
                part_copy(n, which, side).wait_send()
        for row in range(2):
            stat_copy(n, row).wait_send()
        query_copy(n).wait_send()
        for array in range(3):
            wait_bytes(qb.at[0, pl.ds(0, 3 * PIECE)], out_send.at[n, array])
        return carry

    lax.fori_loop(0, STEPS, drain, 0)
    for array in range(3):
        wait_bytes(results[array][1], out_recv.at[array])


def per_device(queries, keys, values, grad_out, neighbours):
    vmem, sem = pltpu.VMEM, pltpu.SemaphoreType.DMA
    out = vmem(queries.shape, bf16)
    anywhere = pl.BlockSpec(memory_space=pl.ANY)
    tokens, result = vmem((STEPS, 4 * TILE, D), bf16), vmem((STEPS, 2, TILE, D), bf16)
    scores, sums = vmem((2, 3, TILE, ROW), f32), vmem((STEPS, 4 * TILE, D), f32)
    stats, parts = vmem((STEPS, 2, 3, ROW), f32), vmem((STEPS, 2, 2, TILE, D), bf16)
    return pl.pallas_call(
        kernel,
        out_shape=(out, out, out),
        in_specs=[anywhere] * 5,
        out_specs=(pl.BlockSpec(memory_space=vmem),) * 3,
        scratch_shapes=[
            tokens, tokens, tokens, tokens,
            vmem((2,) + neighbours.shape, jnp.int32),
            vmem((D, 4 * TILE), bf16),
            scores, scores,
            vmem((2, 3, ROW), f32),
            sums, sums,
            stats, stats,
            parts, parts,
            vmem((ROW, D), f32),
            vmem((STEPS, 2, TILE, D), f32),
            result, result,
            result, result, result,
            sem((3,)),
            sem((STEPS, 8)),
            sem((STEPS, 4)),
            sem((STEPS, 2)),
            sem((STEPS, 4)),
            sem((STEPS, 4)),
            sem((2, STEPS, 2)),
            sem((STEPS, 4)),
            sem((STEPS, 4)),
            sem((2, STEPS)),
            sem((3,)),
            sem((STEPS, 3)),
            pltpu.SemaphoreType.REGULAR,
        ],
        compiler_params=pltpu.CompilerParams(
            collective_id=0, has_side_effects=True, vmem_limit_bytes=56 << 20
        ),
        cost_estimate=pl.CostEstimate(
            flops=13_600_000_000, bytes_accessed=16_000_000, transcendentals=10_600_000
        ),
    )(queries, keys, values, grad_out, neighbours)


def solution(mesh):
    tokens = P(("frame", "head"), None)
    return jax.shard_map(
        per_device,
        mesh=mesh,
        in_specs=(tokens, tokens, tokens, tokens, P("frame", None)),
        out_specs=(tokens, tokens, tokens),
        check_vma=False,
    )
```

```python
import functools

import jax
import jax.numpy as jnp
from jax import lax
from jax.experimental import pallas as pl
from jax.experimental.pallas import tpu as pltpu
from jax.sharding import PartitionSpec as P

D = 128
TILE = 384
ROW = 2 * TILE
PIECE = TILE // 2
STEPS = 6
RING = 4
SCALE = D**-0.5
LOG2E = 1.4426950408889634
ABSENT = -1e30
f32 = jnp.float32
bf16 = jnp.bfloat16
MESH = pl.DeviceIdType.MESH


def dot(a, b, dim_a, dim_b):
    return lax.dot_general(a, b, (((dim_a,), (dim_b,)), ((), ())), preferred_element_type=f32)


def wait_bytes(ref, sem):
    pltpu.make_async_copy(ref, ref, sem).wait()


def remote(src, dst, send_sem, recv_sem, device):
    return pltpu.make_async_remote_copy(
        src_ref=src, dst_ref=dst, send_sem=send_sem, recv_sem=recv_sem, device_id=device,
        device_id_type=MESH,
    )


def rows_at(start, size):
    return pl.ds(pl.multiple_of(start, PIECE), size)


def kernel(
    q_in, k_in, v_in, o_in, near_in,
    q_out, k_out, v_out,
    kb, vb, qb, ob, near, kt, expon, dprob, tops, k_acc, v_acc,
    stat_out, stat_in, part_out, part_in, q_acc, q_keep, q_part, q_other, q_res, k_res, v_res,
    near_sem, in_recv, in_send, fwd_send, halo_recv, halo_send, stat_sem,
    part_recv, part_send, q_sem, out_recv, out_send, entered,
):
    frame, head = lax.axis_index("frame"), lax.axis_index("head")
    group, low = frame // 2, frame % 2
    groups = lax.axis_size("frame") // 2
    x, core = (head // 2) * 2 + low, head % 2
    peer = 1 - core

    def device(chip, which_core):
        return (group * 2 + chip % 2, (chip // 2) * 2 + which_core)

    def places(n):
        parity = (x + n) % 2
        partner = (x + 5 - 2 * parity) % RING
        outer = (x + 3 + 2 * parity) % RING
        mine = (x + RING - parity) % RING
        theirs = (outer + RING - 1 + parity) % RING
        return partner, outer, mine, theirs

    def columns(pair, which_core, n):
        return pl.ds(pl.multiple_of((pair * STEPS + which_core * 3 + n // 2) * D, D), D)

    def tile_slot(chip):
        return (chip % 2) * 2 + chip // 2

    prev_device = (lax.rem(group + groups - 1, groups) * 2 + low, head)
    next_device = (lax.rem(group + 1, groups) * 2 + low, head)
    after, before = (x + 1) % RING, (x + 3) % RING

    barrier = pltpu.get_barrier_semaphore()
    other = device(x, peer)
    for chip in (after, before):
        pl.semaphore_signal(barrier, inc=1, device_id=device(chip, 0), device_id_type=MESH)
    for there in (prev_device, next_device):
        pl.semaphore_signal(
            barrier, inc=1, device_id=(there[0], head + 1 - core), device_id_type=MESH
        )

    @pl.when(core == 0)
    def _():
        pl.semaphore_signal(barrier, inc=1, device_id=other, device_id_type=MESH)
        pl.semaphore_wait(barrier, 5)
        pl.semaphore_signal(entered, inc=1, device_id=other, device_id_type=MESH)

    @pl.when(core == 1)
    def _():
        pl.semaphore_signal(barrier, inc=1, device_id=other, device_id_type=MESH)
        pl.semaphore_wait(entered, 1)

    def wait_groups():
        @pl.when(core == 1)
        def _():
            pl.semaphore_wait(barrier, 5)
            pl.semaphore_signal(entered, inc=1, device_id=other, device_id_type=MESH)

        @pl.when(core == 0)
        def _():
            pl.semaphore_wait(entered, 1)

    key_start = (1 + low) * TILE + core * PIECE
    query_start = tile_slot(x) * TILE + core * PIECE
    inputs = ((k_in, kb, key_start), (v_in, vb, key_start), (q_in, qb, query_start), (o_in, ob, query_start))

    def far_inputs(n, array):
        _, outer, _, theirs = places(n)
        src, dst, start = inputs[array]
        got = in_recv.at[n, 2 * array + low if array < 2 else 2 + array]
        for c in range(2):
            remote(
                src.at[:, columns(theirs, c, n)],
                dst.at[n, rows_at(start, PIECE)],
                in_send.at[n, array],
                got,
                device(outer, c),
            ).start()

    def near_inputs(n, array):
        partner, _, mine, _ = places(n)
        src, dst, start = inputs[array]
        into, sent = dst.at[n, rows_at(start, PIECE)], in_send.at[n, array]
        got = in_recv.at[n, 2 * array + low if array < 2 else 4 + array]
        if array >= 2:
            for c in range(2):
                remote(src.at[:, columns(mine, c, n)], into, sent, got, device(partner, c)).start()
        remote(src.at[:, columns(mine, peer, n)], into, sent, got, device(x, peer)).start()
        pltpu.make_async_copy(src.at[:, columns(mine, core, n)], into, got).start()

    def forward_copy(n, which):
        partner, outer, _, _ = places(n)
        there = (qb, ob)[which].at[n, rows_at(tile_slot(outer) * TILE, TILE)]
        return there, remote(
            there, there, fwd_send.at[n, which], in_recv.at[n, 6 + which], device(partner, core)
        )

    def forward(n, which):
        tile, copy = forward_copy(n, which)
        wait_bytes(tile, in_recv.at[n, 4 + which])
        copy.start()

    def halo_copy(n, which, side):
        buffer = (kb, vb)[which]
        return remote(
            buffer.at[n, pl.ds(TILE * (1 + side), TILE)],
            buffer.at[n, pl.ds(TILE * 3 * (1 - side), TILE)],
            halo_send.at[n, 2 * which + side],
            halo_recv.at[n, 2 * which + side],
            (prev_device, next_device)[side],
        )

    def send_halo(n, which):
        for side in range(2):
            wait_bytes(
                (kb, vb)[which].at[n, pl.ds(TILE * (1 + side), TILE)],
                in_recv.at[n, 2 * which + side],
            )
            halo_copy(n, which, side).start()

    def wait_step(n):
        for which in range(2):
            wait_bytes((qb, ob)[which].at[n, pl.ds(0, 3 * TILE)], in_recv.at[n, 6 + which])
        for which in range(2):
            for side in range(2):
                halo_copy(n, which, side).wait_recv()

    def stat_copy(n, row):
        partner, _, _, _ = places(n)
        return remote(
            stat_out.at[n, row], stat_in.at[n, row], stat_sem.at[0, n, row], stat_sem.at[1, n, row],
            device(partner, core),
        )

    def query_copy(n):
        partner, _, _, _ = places(n)
        return remote(
            q_part.at[n], q_other.at[n], q_sem.at[0, n], q_sem.at[1, n], device(partner, core)
        )

    def part_copy(n, which, side):
        return remote(
            part_out.at[n, which, side],
            part_in.at[n, which, side],
            part_send.at[n, 2 * which + side],
            part_recv.at[n, 2 * which + side],
            (prev_device, next_device)[side],
        )

    def send_parts(n):
        for which in range(2):
            for side in range(2):
                part = (k_acc, v_acc)[which][n, TILE * 3 * side : TILE * 3 * side + TILE, :]
                if which == 0:
                    part = part * SCALE
                part_out[n, which, side] = part.astype(bf16)
                part_copy(n, which, side).start()

    results = ((q_res, q_out), (k_res, k_out), (v_res, v_out))

    def send_result(n, array):
        _, outer, mine, _ = places(n)
        src, dst = results[array]
        into = dst.at[:, columns(mine, core, n)]
        sent, got = out_send.at[n, array], out_recv.at[array]
        for c in range(2):
            remote(
                src.at[n, 1 - low, pl.ds(c * PIECE, PIECE)], into, sent, got, device(outer, c)
            ).start()
        remote(
            src.at[n, low, rows_at(peer * PIECE, PIECE)], into, sent, got, device(x, peer)
        ).start()
        pltpu.make_async_copy(src.at[n, low, rows_at(core * PIECE, PIECE)], into, got).start()

    def finish_queries(n):
        query_copy(n).wait_recv()
        for row in range(2):
            q_res[n, row] = (q_keep[n, row] + q_other[n, row].astype(f32)).astype(bf16)
        send_result(n, 0)

    def finish_keys(n, which):
        for side in range(2):
            part_copy(n, which, side).wait_recv()
            slot = 2 - side
            total = (k_acc, v_acc)[which][n, TILE * slot : TILE * slot + TILE, :]
            if which == 0:
                total = total * SCALE
            total = total + part_in[n, which, side].astype(f32)
            (k_res, v_res)[which][n, slot - 1] = total.astype(bf16)
        send_result(n, 1 + which)

    def keys_at(row, slot):
        return pl.ds(pl.multiple_of((row + slot) * TILE, TILE), TILE)

    def first_half(n, row):
        queries = qb[n, rows_at(row * ROW, ROW), :]
        grads = ob[n, rows_at(row * ROW, ROW), :]
        listed = near[row, 0:1, :]
        bias = [
            jnp.where(listed[:, 1:2] >= 0, 0.0, ABSENT).astype(f32),
            None,
            jnp.where(listed[:, 7:8] >= 0, 0.0, ABSENT).astype(f32),
        ]
        peaks, sums, dots = [], [], []
        for slot in range(3):
            scores = dot(kb[n, keys_at(row, slot), :], queries, 1, 1)
            dprobs = dot(vb[n, keys_at(row, slot), :], grads, 1, 1)
            peak = jnp.max(scores, axis=0, keepdims=True)
            weights = jnp.exp2((scores - peak) * (SCALE * LOG2E))
            sums.append(jnp.sum(weights, axis=0, keepdims=True))
            dots.append(jnp.sum(weights * dprobs, axis=0, keepdims=True))
            expon[row, slot] = weights
            dprob[row, slot] = dprobs
            if bias[slot] is not None:
                peak = peak + bias[slot]
            tops[row, slot : slot + 1, :] = peak
            peaks.append(peak)
        top = functools.reduce(jnp.maximum, peaks)
        factors = [jnp.exp2((peak - top) * (SCALE * LOG2E)) for peak in peaks]
        stat_out[n, row, 0:1, :] = top
        stat_out[n, row, 1:2, :] = functools.reduce(jnp.add, [f * s for f, s in zip(factors, sums)])
        stat_out[n, row, 2:3, :] = functools.reduce(jnp.add, [f * s for f, s in zip(factors, dots)])

    def second_half(n, row):
        queries = qb[n, rows_at(row * ROW, ROW), :]
        grads = ob[n, rows_at(row * ROW, ROW), :]
        here, there = stat_out[n, row], stat_in[n, row]
        top = jnp.maximum(here[0:1], there[0:1])
        factor_here = jnp.exp2((here[0:1] - top) * (SCALE * LOG2E))
        factor_there = jnp.exp2((there[0:1] - top) * (SCALE * LOG2E))
        inverse = 1.0 / (factor_here * here[1:2] + factor_there * there[1:2])
        row_dot = (factor_here * here[2:3] + factor_there * there[2:3]) * inverse
        query_grad = jnp.zeros((D, ROW), f32)
        for slot in range(3):
            factor = jnp.exp2((tops[row, slot : slot + 1, :] - top) * (SCALE * LOG2E)) * inverse
            probs = expon[row, slot] * factor
            dscores = (probs * (dprob[row, slot] - row_dot)).astype(bf16)
            v_acc[n, keys_at(row, slot), :] += dot(probs.astype(bf16), grads, 1, 0)
            k_acc[n, keys_at(row, slot), :] += dot(dscores, queries, 1, 0)
            query_grad += dot(kt[:, keys_at(row, slot)], dscores, 1, 0)
        q_acc[...] = (query_grad * SCALE).T
        _, outer, _, _ = places(n)
        column = jnp.where(row == low, x // 2, outer // 2)
        q_keep[n, row] = q_acc[rows_at(column * TILE, TILE), :]
        q_part[n, row] = q_acc[rows_at((1 - column) * TILE, TILE), :].astype(bf16)

    near_copy = remote(near_in, near.at[low], near_sem.at[0], near_sem.at[1], device(after, core))
    own_near = pltpu.make_async_copy(near_in, near.at[low], near_sem.at[2])

    far_inputs(1, 2)
    far_inputs(0, 1)
    near_copy.start()
    own_near.start()
    far_inputs(0, 0)
    far_inputs(0, 2)
    near_inputs(0, 2)
    near_inputs(5, 0)
    far_inputs(0, 3)
    far_inputs(1, 1)
    near_inputs(0, 3)
    far_inputs(2, 1)
    near_inputs(0, 1)
    near_inputs(4, 0)
    near_inputs(0, 0)
    near_inputs(3, 0)
    far_inputs(2, 0)
    near_inputs(2, 0)
    k_acc[...] = jnp.zeros_like(k_acc)
    v_acc[...] = jnp.zeros_like(v_acc)
    wait_groups()
    send_halo(0, 1)
    near_inputs(1, 3)
    near_inputs(3, 1)
    far_inputs(1, 3)
    send_halo(0, 0)
    forward(0, 0)
    near_inputs(1, 1)
    forward(0, 1)
    near_inputs(4, 1)
    near_inputs(1, 2)
    far_inputs(2, 2)
    near_inputs(2, 1)
    send_halo(1, 1)
    forward(1, 0)
    far_inputs(1, 0)
    near_inputs(1, 0)
    send_halo(2, 1)
    near_inputs(5, 1)
    send_halo(2, 0)
    forward(1, 1)
    far_inputs(2, 3)
    far_inputs(4, 1)
    far_inputs(3, 0)
    near_copy.wait()
    own_near.wait()

    def step(n, carry):
        wait_step(n)
        kt[...] = kb[n].T

        def first(row, inner):
            first_half(n, row)
            stat_copy(n, row).start()

            @pl.when(jnp.logical_and(n == 0, row == 0))
            def _():
                far_inputs(3, 1)
                far_inputs(4, 2)
                send_halo(1, 0)

            @pl.when(jnp.logical_and(n == 1, row == 0))
            def _():
                forward(2, 0)

            @pl.when(jnp.logical_and(n == 2, row == 0))
            def _():
                far_inputs(5, 3)
                send_halo(4, 0)

            @pl.when(jnp.logical_and(n == 3, row == 0))
            def _():
                finish_keys(0, 1)

            return inner

        lax.fori_loop(0, 2, first, 0)

        @pl.when(n == 0)
        def _():
            far_inputs(3, 3)
            near_inputs(2, 3)
            send_halo(3, 0)
            near_inputs(2, 2)

        @pl.when(n == 1)
        def _():
            forward(2, 1)
            far_inputs(3, 2)
            far_inputs(4, 0)
            forward(3, 1)
            far_inputs(4, 3)
            far_inputs(5, 0)
            near_inputs(3, 3)
            near_inputs(3, 2)

        @pl.when(n == 2)
        def _():
            forward(3, 0)
            send_halo(5, 1)
            forward(4, 0)
            send_halo(4, 1)
            near_inputs(4, 3)
            near_inputs(5, 2)
            send_halo(5, 0)
            near_inputs(4, 2)
            far_inputs(5, 2)

        @pl.when(n == 3)
        def _():
            query_copy(1).start()
            finish_keys(0, 0)
            finish_keys(1, 1)
            near_inputs(5, 3)

        @pl.when(n == 4)
        def _():
            query_copy(3).start()
            finish_queries(1)
            finish_keys(2, 1)
            query_copy(2).start()
            finish_keys(1, 0)

        @pl.when(n == 5)
        def _():
            query_copy(4).start()
            finish_queries(2)
            finish_keys(3, 1)
            finish_keys(2, 0)
            finish_queries(0)

        def second(row, inner):
            stat_copy(n, row).wait_recv()
            second_half(n, row)

            @pl.when(jnp.logical_and(n == 0, row == 0))
            def _():
                far_inputs(5, 1)
                send_halo(3, 1)

            @pl.when(jnp.logical_and(n == 2, row == 0))
            def _():
                forward(4, 1)
                forward(5, 1)
                query_copy(0).start()

            @pl.when(jnp.logical_and(n == 3, row == 0))
            def _():
                forward(5, 0)

            return inner

        lax.fori_loop(0, 2, second, 0)
        send_parts(n)

        return carry

    lax.fori_loop(0, STEPS, step, 0)
    finish_keys(3, 0)
    query_copy(5).start()
    finish_keys(4, 1)
    finish_keys(4, 0)
    finish_queries(3)
    finish_keys(5, 0)
    finish_keys(5, 1)
    finish_queries(5)
    finish_queries(4)

    def drain(n, carry):
        for array in range(4):
            wait_bytes(qb.at[0, pl.ds(0, (3 if array < 2 else 5) * PIECE)], in_send.at[n, array])
        for which in range(2):
            forward_copy(n, which)[1].wait_send()
            for side in range(2):
                halo_copy(n, which, side).wait_send()
                part_copy(n, which, side).wait_send()
        for row in range(2):
            stat_copy(n, row).wait_send()
        query_copy(n).wait_send()
        for array in range(3):
            wait_bytes(qb.at[0, pl.ds(0, 3 * PIECE)], out_send.at[n, array])
        return carry

    lax.fori_loop(0, STEPS, drain, 0)
    for array in range(3):
        wait_bytes(results[array][1], out_recv.at[array])


def store_kernel(q_from, k_from, v_from, q_to, k_to, v_to, sems):
    pairs = ((q_from, q_to), (k_from, k_to), (v_from, v_to))
    copies = []
    for i, (src, dst) in enumerate(pairs):
        for part in range(4):
            rows = pl.ds(part * PIECE // 4, PIECE // 4)
            copies.append(pltpu.make_async_copy(src.at[rows], dst.at[rows], sems.at[i, part]))
    for copy in copies:
        copy.start()
    for copy in copies:
        copy.wait()


def per_device(queries, keys, values, grad_out, neighbours):
    vmem, sem = pltpu.VMEM, pltpu.SemaphoreType.DMA
    out = vmem(queries.shape, bf16)
    anywhere = pl.BlockSpec(memory_space=pl.ANY)
    tokens, result = vmem((STEPS, 4 * TILE, D), bf16), vmem((STEPS, 2, TILE, D), bf16)
    scores, sums = vmem((2, 3, TILE, ROW), f32), vmem((STEPS, 4 * TILE, D), f32)
    stats, parts = vmem((STEPS, 2, 3, ROW), f32), vmem((STEPS, 2, 2, TILE, D), bf16)
    placed = pl.pallas_call(
        kernel,
        out_shape=(out, out, out),
        in_specs=[anywhere] * 5,
        out_specs=(pl.BlockSpec(memory_space=vmem),) * 3,
        scratch_shapes=[
            tokens, tokens, tokens, tokens,
            vmem((2,) + neighbours.shape, jnp.int32),
            vmem((D, 4 * TILE), bf16),
            scores, scores,
            vmem((2, 3, ROW), f32),
            sums, sums,
            stats, stats,
            parts, parts,
            vmem((ROW, D), f32),
            vmem((STEPS, 2, TILE, D), f32),
            result, result,
            result, result, result,
            sem((3,)),
            sem((STEPS, 8)),
            sem((STEPS, 4)),
            sem((STEPS, 2)),
            sem((STEPS, 4)),
            sem((STEPS, 4)),
            sem((2, STEPS, 2)),
            sem((STEPS, 4)),
            sem((STEPS, 4)),
            sem((2, STEPS)),
            sem((3,)),
            sem((STEPS, 3)),
            pltpu.SemaphoreType.REGULAR,
        ],
        compiler_params=pltpu.CompilerParams(
            collective_id=0, has_side_effects=True, vmem_limit_bytes=56 << 20
        ),
        cost_estimate=pl.CostEstimate(
            flops=13_600_000_000, bytes_accessed=16_000_000, transcendentals=10_600_000
        ),
    )(queries, keys, values, grad_out, neighbours)
    placed = [pltpu.with_memory_space_constraint(array, pltpu.VMEM) for array in placed]
    out = jax.ShapeDtypeStruct(queries.shape, bf16)
    return pl.pallas_call(
        store_kernel,
        out_shape=(out, out, out),
        in_specs=[anywhere] * 3,
        out_specs=(anywhere,) * 3,
        scratch_shapes=[sem((3, 4))],
    )(*placed)


def solution(mesh):
    tokens = P(("frame", "head"), None)
    return jax.shard_map(
        per_device,
        mesh=mesh,
        in_specs=(tokens, tokens, tokens, tokens, P("frame", None)),
        out_specs=(tokens, tokens, tokens),
        check_vma=False,
    )
```
